32 devices in a mesh: band: 4 (over z), row: 8 (over y, x, core).
Axes of the slice: x: 2, y: 2, z: 4, core: 2. Of those that a mesh axis runs over, the one named last changes fastest.
Arguments:
- recorded: bfloat16 [1024, 1024, 512], P(('row', 'band')), may hold values from -5 to 5
- acquired: int32 [128, 128], replicated, may hold values 0 or 1
- partner: int32 [128], replicated, may hold values from 0 to 127, each once
- band_counts: int32 [4], replicated, may hold values from 1 to 12, 32 in all
- wavelet: float32 [2, 4], replicated, may hold values from -0.75 to 0.75, as said below
Outputs:
- primaries: bfloat16 [1024, 1024, 512], P(('row', 'band'))
The draws below stay inside these ranges and needn't reach their ends.
Inputs may be any that keep to these rules, and one draw needn't show every extreme that they name: `partner`: a permutation of the 128 block indices. `band_counts`: the counts sum to 32; the largest is exactly 12. `wavelet`: each column, read as a complex number, has magnitude between 0.55 and 0.75.
All inputs are finite; a program needn't handle non-finite values.
Results may differ from the reference program's by a relative error of at most 0.0085.
Values may be sent and summed in bfloat16 or wider, within the bound.
A program may use at most 256 MiB of HBM per device.

```python
import math
import jax
import jax.numpy as jnp
import numpy as np
from jax import lax

NS = 1024
NT = 512
NF = 32
FLO = 4
BS = 8
ITERS = 5
NB = 128
NGROUPS = 4
CAP = 12


def draw_recorded(key, part):
    normal_part = jax.random.normal(key, (NS, NS, NT), jnp.float32)
    return jnp.clip(normal_part, -5.0, 5.0).astype(jnp.bfloat16)


def draw_wavelet(key, part):
    first_key, second_key = jax.random.split(jax.random.fold_in(key, 17))
    magnitude = jax.random.uniform(first_key, (NGROUPS,), jnp.float32, 0.55, 0.75)
    turning = jax.random.uniform(second_key, (NGROUPS,), jnp.float32, -math.pi, math.pi)
    return jnp.stack([magnitude * jnp.cos(turning), magnitude * jnp.sin(turning)], axis=0)


def touch_ends(entries, own_key, smallest, top_value):
    extent = entries.shape
    index_at = [jax.random.randint(jax.random.fold_in(own_key, axis), (), 0, extent[axis]) for axis in range(len(extent))]
    entries = entries.at[tuple(index_at)].set(smallest)
    longest = extent.index(max(extent))
    index_at[longest] = (index_at[longest] + 1) % extent[longest]
    return entries.at[tuple(index_at)].set(top_value)


def profile(number_of, total, most, skew):
    weights = [(1 << 20) // math.isqrt(standing ** skew) + 1 for standing in range(2, number_of + 1)]
    rest, counts = total - most - (number_of - 1), [1] * (number_of - 1)
    while rest > 0:
        movable = [i for i in range(number_of - 1) if counts[i] < most]
        mass, left = sum([weights[i] for i in movable]), rest
        for i in movable:
            extra = min(most - counts[i], max(1, left * weights[i] // mass), rest)
            counts[i] = counts[i] + extra
            rest = rest - extra
    return np.array([most] + counts)


def ragged(key, count, total, most, skew):
    if count == 2:
        one = jax.random.randint(key, (), max(1, total - most), min(most, total - 1) + 1)
        return jnp.stack([one, total - one])
    sizes = jnp.asarray(profile(count, total, most, skew), jnp.int32)
    twos = (count - 1) // 2
    source_of, sink = sizes[1:1 + 2 * twos:2], sizes[2:2 + 2 * twos:2]
    room = jnp.minimum(source_of - 1, most - sink)
    moved = jax.random.randint(jax.random.fold_in(key, 1), (twos,), 0, 1 << 20) % (room + 1)
    sizes = sizes.at[1:1 + 2 * twos:2].set(source_of - moved).at[2:2 + 2 * twos:2].set(sink + moved)
    return sizes[jax.random.permutation(jax.random.fold_in(key, 2), count)]


def setup_inputs(seed: int = 0) -> dict:
    arg_keys = jax.random.split(jax.random.key(seed), 6)
    return {
        "recorded": draw_recorded(jax.random.fold_in(arg_keys[5], 71), 0),
        "acquired": touch_ends((jax.random.randint(arg_keys[1], (NB, NB), 0, 4) < 3).astype(jnp.int32), jax.random.fold_in(arg_keys[1], 1), 0, 1),
        "partner": jax.random.permutation(arg_keys[2], NB).astype(jnp.int32),
        "band_counts": ragged(arg_keys[3], NGROUPS, NF, CAP, 2).astype(jnp.int32),
        "wavelet": draw_wavelet(jax.random.fold_in(arg_keys[5], 71), 0),
    }


def dft_tables():
    sample_index = jnp.arange(NT, dtype=jnp.int32)
    bin_index = FLO + jnp.arange(NF, dtype=jnp.int32)
    angles = (bin_index[:, None] * sample_index[None, :] % NT).astype(jnp.float32) * (2.0 * math.pi / NT)
    cycles = jnp.concatenate([jnp.cos(angles), -jnp.sin(angles)], axis=0)
    forward = (cycles * (1.0 / math.sqrt(NT))).astype(jnp.bfloat16)
    inverse = (cycles * math.sqrt(2.0 / NF)).astype(jnp.bfloat16)
    return (forward, inverse)

def reference(recorded, acquired, partner, band_counts, wavelet):
    forward, inverse = dft_tables()
    block_rows = min(32, NS)
    block_total = NS // block_rows
    forward_wide = forward.astype(jnp.float32)
    inverse_wide = inverse.astype(jnp.float32)

    def transform(shot_block):
        return jnp.einsum('ct,srt->csr', forward_wide, shot_block.astype(jnp.float32), precision=lax.Precision.HIGHEST).astype(jnp.bfloat16)
    spectra = lax.map(transform, recorded.reshape(block_total, block_rows, NS, NT))
    spectra = jnp.moveaxis(spectra, 1, 0).reshape(2 * NF, NS, NS)
    offsets = jnp.arange(BS, dtype=jnp.int32)
    mirror_index = (BS * partner[:, None] + offsets[None, :]).reshape(NS).astype(jnp.int32)
    present = jnp.repeat(jnp.repeat(acquired, BS, axis=0), BS, axis=1) == 1
    mirrored = jnp.take(jnp.take(spectra, mirror_index, axis=1), mirror_index, axis=2)
    filled = jnp.where(present[None], spectra, jnp.swapaxes(mirrored, 1, 2))
    band_ends = jnp.cumsum(band_counts).astype(jnp.int32)
    bin_index = jnp.arange(NF, dtype=jnp.int32)
    bin_group = lax.optimization_barrier(jnp.sum((band_ends[None, :] <= bin_index[:, None]).astype(jnp.int32), axis=1))
    rescale = 1.0 / math.sqrt(NS)
    wave_re = wavelet[0][bin_group] * rescale
    wave_im = wavelet[1][bin_group] * rescale

    def solve(items):
        data_re, data_im, scale_re, scale_im = items
        base_re = data_re.astype(jnp.float32)
        base_im = data_im.astype(jnp.float32)
        factor_re = (scale_re * base_re - scale_im * base_im).astype(jnp.bfloat16)
        factor_im = (scale_re * base_im + scale_im * base_re).astype(jnp.bfloat16)
        factor_re, factor_im = lax.optimization_barrier((factor_re, factor_im))
        wide_fre = factor_re.astype(jnp.float32)
        wide_fim = factor_im.astype(jnp.float32)
        left_re, left_im = (data_re, data_im)
        for sweep_turn in range(ITERS):
            wide_lre = left_re.astype(jnp.float32)
            wide_lim = left_im.astype(jnp.float32)
            real_part = jnp.dot(wide_lre, wide_fre, precision=lax.Precision.HIGHEST) - jnp.dot(wide_lim, wide_fim, precision=lax.Precision.HIGHEST)
            imag_part = jnp.dot(wide_lre, wide_fim, precision=lax.Precision.HIGHEST) + jnp.dot(wide_lim, wide_fre, precision=lax.Precision.HIGHEST)
            left_re = (base_re - real_part).astype(jnp.bfloat16)
            left_im = (base_im - imag_part).astype(jnp.bfloat16)
            left_re, left_im = lax.optimization_barrier((left_re, left_im))
        return (left_re, left_im)
    estimate_re, estimate_im = lax.map(solve, (filled[:NF], filled[NF:], wave_re, wave_im))
    estimate = jnp.concatenate([estimate_re, estimate_im], axis=0)
    shot_blocks = jnp.moveaxis(estimate.reshape(2 * NF, block_total, block_rows, NS), 1, 0)

    def restore(shot_block):
        return jnp.einsum('csr,ct->srt', shot_block.astype(jnp.float32), inverse_wide, precision=lax.Precision.HIGHEST).astype(jnp.bfloat16)
    return lax.map(restore, shot_blocks).reshape(NS, NS, NT)
```

```python
import math

import jax
import jax.numpy as jnp
from jax import lax
from jax.experimental import pallas as pl
from jax.experimental.pallas import tpu as pltpu
from jax.sharding import PartitionSpec as P

NT = 512
NF = 32
FLO = 4
BS = 8
ITERS = 5
CHUNKS = 2
AXES = ("row", "band")


def dft_tables():
    sample_index = jnp.arange(NT, dtype=jnp.int32)
    bin_index = FLO + jnp.arange(NF, dtype=jnp.int32)
    angles = (bin_index[:, None] * sample_index[None, :] % NT).astype(jnp.float32) * (
        2.0 * math.pi / NT
    )
    cycles = jnp.concatenate([jnp.cos(angles), -jnp.sin(angles)], axis=0)
    forward = (cycles * (1.0 / math.sqrt(NT))).astype(jnp.bfloat16)
    inverse = (cycles * math.sqrt(2.0 / NF)).astype(jnp.bfloat16)
    return (forward, inverse)


def solve_kernel(tile, base_ref, factor_ref, out_ref, held):
    width = base_ref.shape[1]
    for turn in range(ITERS):
        left = base_ref if turn == 0 else held.at[(turn + 1) % 2]
        into = out_ref if turn == ITERS - 1 else held.at[turn % 2]

        @pl.loop(0, width // tile)
        def _(step):
            columns = pl.ds(pl.multiple_of(step * tile, tile), tile)
            product = jnp.dot(
                left[...], factor_ref[:, columns], preferred_element_type=jnp.float32
            )
            into[:, columns] = (base_ref[:, columns].astype(jnp.float32) - product).astype(
                jnp.bfloat16
            )


def solve(base, factor):
    rows, width = base.shape
    tile = min(512, width)
    vmem = pl.BlockSpec(memory_space=pltpu.VMEM)
    return pl.pallas_call(
        lambda *refs: solve_kernel(tile, *refs),
        out_shape=jax.ShapeDtypeStruct((rows, width), jnp.bfloat16),
        in_specs=[vmem, vmem],
        out_specs=vmem,
        scratch_shapes=[pltpu.VMEM((2, rows, width), jnp.bfloat16)],
        compiler_params=pltpu.CompilerParams(vmem_limit_bytes=48 << 20),
        cost_estimate=pl.CostEstimate(
            flops=2 * ITERS * rows * width * width,
            bytes_accessed=2 * (2 * rows * width + width * width),
            transcendentals=0,
        ),
        name="solve",
    )(base, factor)


def restore_kernel(data_ref, table_ref, *rest):
    out_ref = rest[-1]
    out_ref[0] = lax.dot_general(
        data_ref[0], table_ref[...], (((0,), (0,)), ((), ())), preferred_element_type=jnp.float32
    ).astype(jnp.bfloat16)


def restore(data, table, whole, first, shot_count):
    count, parts, stations = data.shape
    samples = table.shape[1]
    in_specs = [
        pl.BlockSpec((1, parts, stations), lambda i: (i, 0, 0)),
        pl.BlockSpec((parts, samples), lambda i: (0, 0)),
    ]
    args = [data, table]
    aliases = {}
    if whole is not None:
        in_specs.append(pl.BlockSpec(memory_space=pl.ANY))
        args.append(whole)
        aliases = {2: 0}
    return pl.pallas_call(
        restore_kernel,
        grid=(count,),
        out_shape=jax.ShapeDtypeStruct((shot_count, stations, samples), jnp.bfloat16),
        in_specs=in_specs,
        out_specs=pl.BlockSpec((1, stations, samples), lambda i: (first + i, 0, 0)),
        input_output_aliases=aliases,
        compiler_params=pltpu.CompilerParams(vmem_limit_bytes=32 << 20),
        cost_estimate=pl.CostEstimate(
            flops=2 * count * parts * stations * samples,
            bytes_accessed=2 * count * stations * (samples + parts),
            transcendentals=0,
        ),
        name="restore",
    )(*args)


def shards(recorded, acquired, partner, band_counts, wavelet):
    band_size = lax.axis_size("band")
    devices = band_size * lax.axis_size("row")
    shot_count, stations, _ = recorded.shape
    copies = devices // NF
    here = lax.axis_index("row") * band_size + lax.axis_index("band")
    forward, inverse = dft_tables()

    chunks = min(CHUNKS, shot_count // copies)
    size = shot_count // chunks
    pieces = []
    for chunk in range(chunks):
        part = lax.slice_in_dim(recorded, chunk * size, (chunk + 1) * size, axis=0)
        spectra = jnp.einsum(
            "ct,srt->csr", forward, part, preferred_element_type=jnp.float32
        ).astype(jnp.bfloat16)
        spectra = jnp.swapaxes(spectra.reshape(2, NF, size, stations), 0, 1)
        if copies > 1:
            spectra = jnp.repeat(spectra, copies, axis=0)
        pieces.append(lax.all_to_all(spectra, AXES, split_axis=0, concat_axis=0, tiled=True))
    data = jnp.stack(pieces, axis=2)
    data = jnp.swapaxes(data, 0, 1).reshape(2, stations, stations)

    offsets = jnp.arange(BS, dtype=jnp.int32)
    mirror_index = (BS * partner[:, None] + offsets[None, :]).reshape(stations)
    station = jnp.arange(stations, dtype=jnp.int32)
    permute = (mirror_index[:, None] == station[None, :]).astype(jnp.bfloat16)
    present = jnp.repeat(jnp.repeat(acquired, BS, axis=0), BS, axis=1) == 1
    filled = []
    for part in range(2):
        moved = jnp.dot(permute, data[part], preferred_element_type=jnp.float32)
        mirrored = lax.dot_general(
            permute,
            moved.astype(jnp.bfloat16),
            (((1,), (1,)), ((), ())),
            preferred_element_type=jnp.float32,
        ).astype(jnp.bfloat16)
        filled.append(jnp.where(present, data[part], mirrored))
    base_re, base_im = filled
    own_bin = here // copies
    own_group = jnp.sum((jnp.cumsum(band_counts) <= own_bin).astype(jnp.int32))
    chosen = (jnp.arange(band_counts.shape[0], dtype=jnp.int32) == own_group).astype(jnp.float32)
    rescale = 1.0 / math.sqrt(stations)
    wave_re = jnp.sum(chosen * wavelet[0]) * rescale
    wave_im = jnp.sum(chosen * wavelet[1]) * rescale
    wide_re = base_re.astype(jnp.float32)
    wide_im = base_im.astype(jnp.float32)
    factor_re = (wave_re * wide_re - wave_im * wide_im).astype(jnp.bfloat16)
    factor_im = (wave_re * wide_im + wave_im * wide_re).astype(jnp.bfloat16)
    factor = jnp.concatenate(
        [
            jnp.concatenate([factor_re, factor_im], axis=1),
            jnp.concatenate([-factor_im, factor_re], axis=1),
        ],
        axis=0,
    )
    base = jnp.concatenate([base_re, base_im], axis=1)

    own_count = shot_count // copies
    base = base.reshape(devices, shot_count, 2 * stations)
    if copies > 1:
        base = lax.dynamic_slice_in_dim(base, here % copies * own_count, own_count, axis=1)
    size = own_count // chunks
    output = None
    for chunk in range(chunks):
        rows = lax.slice_in_dim(base, chunk * size, (chunk + 1) * size, axis=1)
        solved = solve(rows.reshape(devices * size, 2 * stations), factor)
        solved = solved.reshape(devices, size, 2 * stations)
        back = lax.all_to_all(solved, AXES, split_axis=0, concat_axis=0, tiled=True)
        back = back.reshape(NF, copies, size, 2, stations)
        back = jnp.transpose(back, (1, 2, 3, 0, 4)).reshape(copies, size, 2 * NF, stations)
        for copy in range(copies):
            output = restore(
                back[copy], inverse, output, copy * own_count + chunk * size, shot_count
            )
    return output


def solution(mesh):
    return jax.shard_map(
        shards,
        mesh=mesh,
        in_specs=(P(AXES, None, None), P(), P(), P(), P()),
        out_specs=P(AXES, None, None),
        check_vma=False,
    )
```

```python
import math

import jax
import jax.numpy as jnp
import numpy as np
from jax import lax
from jax.experimental import pallas as pl
from jax.experimental.pallas import tpu as pltpu
from jax.sharding import PartitionSpec as P

NT = 512
NF = 32
FLO = 4
BS = 8
ITERS = 5
CHUNKS = 4
AXES = ("row", "band")


def dft_tables():
    sample_index = np.arange(NT, dtype=np.int32)
    bin_index = FLO + np.arange(NF, dtype=np.int32)
    angles = (bin_index[:, None] * sample_index[None, :] % NT).astype(np.float32) * np.float32(
        2.0 * math.pi / NT
    )
    cycles = np.concatenate([np.cos(angles), -np.sin(angles)], axis=0)
    forward = cycles * np.float32(1.0 / math.sqrt(NT))
    inverse = cycles * np.float32(math.sqrt(2.0 / NF))
    return (jnp.asarray(forward, jnp.bfloat16), jnp.asarray(inverse, jnp.bfloat16))


def fill_kernel(
    partner_ref, wave_ref, data_ref, permute_ref, mask_ref, base_ref, factor_ref, turned, taken
):
    stations = data_ref.shape[1]
    block = min(128, stations)
    for part in range(2):

        @pl.loop(0, stations // block)
        def _(step):
            rows = pl.ds(pl.multiple_of(step * block, block), block)
            turned[:, rows] = data_ref[part, rows, :].astype(jnp.float32).T

        @pl.loop(0, stations // BS)
        def _(step):
            source = pl.ds(pl.multiple_of(partner_ref[step] * BS, BS), BS)
            into = pl.ds(pl.multiple_of(step * BS, BS), BS)
            taken[part, into, :] = turned[source, :]

    tile = min(256, stations)
    wave_re = wave_ref[0]
    wave_im = wave_ref[1]

    @pl.loop(0, stations // tile)
    def _(step):
        rows = pl.ds(pl.multiple_of(step * tile, tile), tile)
        lower = pl.ds(pl.multiple_of(stations + step * tile, tile), tile)
        present = mask_ref[rows, :].astype(jnp.float32) > 0.5
        filled = []
        for part in range(2):
            mirrored = jnp.dot(
                taken[part, rows, :].astype(jnp.bfloat16),
                permute_ref[...],
                preferred_element_type=jnp.float32,
            )
            value = jnp.where(present, data_ref[part, rows, :].astype(jnp.float32), mirrored)
            base_ref[rows, part * stations : (part + 1) * stations] = value.astype(jnp.bfloat16)
            filled.append(value)
        factor_re = (wave_re * filled[0] - wave_im * filled[1]).astype(jnp.bfloat16)
        factor_im = (wave_re * filled[1] + wave_im * filled[0]).astype(jnp.bfloat16)
        factor_ref[rows, :stations] = factor_re
        factor_ref[rows, stations:] = factor_im
        factor_ref[lower, :stations] = -factor_im
        factor_ref[lower, stations:] = factor_re


def fill(partner, wave, data, permute, mask):
    stations = data.shape[1]
    vmem = pl.BlockSpec(memory_space=pltpu.VMEM)
    smem = pl.BlockSpec(memory_space=pltpu.SMEM)
    return pl.pallas_call(
        fill_kernel,
        out_shape=(
            jax.ShapeDtypeStruct((stations, 2 * stations), jnp.bfloat16),
            jax.ShapeDtypeStruct((2 * stations, 2 * stations), jnp.bfloat16),
        ),
        in_specs=[smem, smem, vmem, vmem, vmem],
        out_specs=(vmem, vmem),
        scratch_shapes=[
            pltpu.VMEM((stations, stations), jnp.float32),
            pltpu.VMEM((2, stations, stations), jnp.float32),
        ],
        compiler_params=pltpu.CompilerParams(vmem_limit_bytes=56 << 20),
        cost_estimate=pl.CostEstimate(
            flops=4 * stations**3, bytes_accessed=20 * stations**2, transcendentals=0
        ),
        name="fill",
    )(partner, wave, data, permute, mask)


def solve_kernel(tile, base_ref, factor_ref, out_ref, held):
    width = base_ref.shape[1]
    half = width // 2
    for turn in range(ITERS):
        left = base_ref if turn == 0 else held.at[(turn + 1) % 2]

        @pl.loop(0, width // tile)
        def _(step):
            columns = pl.ds(pl.multiple_of(step * tile, tile), tile)
            product = jnp.dot(
                left[...], factor_ref[:, columns], preferred_element_type=jnp.float32
            )
            value = (base_ref[:, columns].astype(jnp.float32) - product).astype(jnp.bfloat16)
            if turn == ITERS - 1:
                inside = pl.ds(pl.multiple_of(step * tile % half, tile), tile)
                out_ref[step * tile // half, :, inside] = value
            else:
                held[turn % 2, :, columns] = value


def solve(base, factor):
    rows, width = base.shape
    tile = min(512, width // 2)
    vmem = pl.BlockSpec(memory_space=pltpu.VMEM)
    return pl.pallas_call(
        lambda *refs: solve_kernel(tile, *refs),
        out_shape=jax.ShapeDtypeStruct((2, rows, width // 2), jnp.bfloat16),
        in_specs=[vmem, vmem],
        out_specs=vmem,
        scratch_shapes=[pltpu.VMEM((2, rows, width), jnp.bfloat16)],
        compiler_params=pltpu.CompilerParams(vmem_limit_bytes=40 << 20),
        cost_estimate=pl.CostEstimate(
            flops=2 * ITERS * rows * width * width,
            bytes_accessed=2 * (2 * rows * width + width * width),
            transcendentals=0,
        ),
        name="solve",
    )(base, factor)


def restore_kernel(data_ref, table_ref, *rest):
    out_ref = rest[-1]
    for shot in range(data_ref.shape[0]):
        out_ref[shot] = lax.dot_general(
            data_ref[shot],
            table_ref[...],
            (((0,), (0,)), ((), ())),
            preferred_element_type=jnp.float32,
        ).astype(jnp.bfloat16)


def restore(data, table, whole, first, shot_count):
    count, parts, stations = data.shape
    samples = table.shape[1]
    step = math.gcd(math.gcd(4, count), first) if first else math.gcd(4, count)
    in_specs = [
        pl.BlockSpec((step, parts, stations), lambda i: (i, 0, 0)),
        pl.BlockSpec((parts, samples), lambda i: (0, 0)),
    ]
    args = [data, table]
    aliases = {}
    if whole is not None:
        in_specs.append(pl.BlockSpec(memory_space=pl.ANY))
        args.append(whole)
        aliases = {2: 0}
    return pl.pallas_call(
        restore_kernel,
        grid=(count // step,),
        out_shape=jax.ShapeDtypeStruct((shot_count, stations, samples), jnp.bfloat16),
        in_specs=in_specs,
        out_specs=pl.BlockSpec((step, stations, samples), lambda i: (first // step + i, 0, 0)),
        input_output_aliases=aliases,
        compiler_params=pltpu.CompilerParams(vmem_limit_bytes=32 << 20),
        cost_estimate=pl.CostEstimate(
            flops=2 * count * parts * stations * samples,
            bytes_accessed=2 * count * stations * (samples + parts),
            transcendentals=0,
        ),
        name="restore",
    )(*args)


def shards(recorded, acquired, partner, band_counts, wavelet):
    band_size = lax.axis_size("band")
    devices = band_size * lax.axis_size("row")
    shot_count, stations, _ = recorded.shape
    copies = devices // NF
    here = lax.axis_index("row") * band_size + lax.axis_index("band")
    forward, inverse = dft_tables()

    head = max(1, shot_count // 4)
    pieces = []
    for begin, end in ((0, head), (head, shot_count)):
        part = lax.slice_in_dim(recorded, begin, end, axis=0)
        spectra = jnp.einsum(
            "ct,srt->csr", forward, part, preferred_element_type=jnp.float32
        ).astype(jnp.bfloat16)
        spectra = jnp.swapaxes(spectra.reshape(2, NF, end - begin, stations), 0, 1)
        if copies > 1:
            spectra = jnp.repeat(spectra, copies, axis=0)
        pieces.append(lax.all_to_all(spectra, AXES, split_axis=0, concat_axis=0, tiled=True))
    data = jnp.concatenate(pieces, axis=2)
    data = jnp.swapaxes(data, 0, 1).reshape(2, stations, stations)

    offsets = jnp.arange(BS, dtype=jnp.int32)
    mirror_index = (BS * partner[:, None] + offsets[None, :]).reshape(stations)
    station = jnp.arange(stations, dtype=jnp.int32)
    permute = (station[:, None] == mirror_index[None, :]).astype(jnp.bfloat16)
    mask = jnp.repeat(jnp.repeat(acquired, BS, axis=0), BS, axis=1).astype(jnp.bfloat16)
    own_bin = here // copies
    own_group = jnp.sum((jnp.cumsum(band_counts) <= own_bin).astype(jnp.int32))
    chosen = jnp.arange(band_counts.shape[0], dtype=jnp.int32) == own_group
    rescale = 1.0 / math.sqrt(stations)
    wave = jnp.sum(chosen.astype(jnp.float32)[None] * wavelet, axis=1) * rescale
    base, factor = fill(partner, wave, data, permute, mask)

    own_count = shot_count // copies
    base = base.reshape(devices, shot_count, 2 * stations)
    if copies > 1:
        base = lax.dynamic_slice_in_dim(base, here % copies * own_count, own_count, axis=1)
    chunks = min(CHUNKS, own_count)
    size = own_count // chunks
    output = None
    for chunk in range(chunks):
        rows = lax.slice_in_dim(base, chunk * size, (chunk + 1) * size, axis=1)
        solved = solve(rows.reshape(devices * size, 2 * stations), factor)
        solved = jnp.swapaxes(solved.reshape(2, devices, size, stations), 0, 1)
        back = lax.all_to_all(solved, AXES, split_axis=0, concat_axis=0, tiled=True)
        if output is not None:
            back, output = lax.optimization_barrier((back, output))
        back = back.reshape(NF, copies, 2, size, stations)
        back = jnp.transpose(back, (1, 3, 2, 0, 4)).reshape(copies, size, 2 * NF, stations)
        for copy in range(copies):
            output = restore(
                back[copy], inverse, output, copy * own_count + chunk * size, shot_count
            )
    return output


def solution(mesh):
    return jax.shard_map(
        shards,
        mesh=mesh,
        in_specs=(P(AXES, None, None), P(), P(), P(), P()),
        out_specs=P(AXES, None, None),
        check_vma=False,
    )
```

```python
import math

import jax
import jax.numpy as jnp
import numpy as np
from jax import lax
from jax.experimental import pallas as pl
from jax.experimental.pallas import tpu as pltpu
from jax.sharding import PartitionSpec as P

NT = 512
NF = 32
FLO = 4
BS = 8
ITERS = 5
CHUNKS = 4
AXES = ("row", "band")


def dft_tables():
    sample_index = np.arange(NT, dtype=np.int32)
    bin_index = FLO + np.arange(NF, dtype=np.int32)
    angles = (bin_index[:, None] * sample_index[None, :] % NT).astype(np.float32) * np.float32(
        2.0 * math.pi / NT
    )
    cycles = np.concatenate([np.cos(angles), -np.sin(angles)], axis=0)
    forward = cycles * np.float32(1.0 / math.sqrt(NT))
    inverse = cycles * np.float32(math.sqrt(2.0 / NF))
    return (jnp.asarray(forward, jnp.bfloat16), jnp.asarray(inverse, jnp.bfloat16))


def iterate(tile, base_ref, factor_ref, out_ref, held):
    width = base_ref.shape[1]
    half = width // 2
    for turn in range(ITERS):
        left = base_ref if turn == 0 else held.at[(turn + 1) % 2]

        @pl.loop(0, width // tile)
        def _(step):
            columns = pl.ds(pl.multiple_of(step * tile, tile), tile)
            product = jnp.dot(
                left[...], factor_ref[:, columns], preferred_element_type=jnp.float32
            )
            value = base_ref[:, columns].astype(jnp.float32) - product
            if turn == ITERS - 1:
                inside = pl.ds(pl.multiple_of(step * tile % half, tile), tile)
                part = step * tile // half
                if len(out_ref.shape) == 4:
                    groups, _, size, _ = out_ref.shape
                    value = value.reshape(groups, size, tile)
                    out_ref[:, part, :, inside] = value.astype(jnp.bfloat16)
                else:
                    out_ref[part, :, inside] = value.astype(jnp.bfloat16)
            else:
                held[turn % 2, :, columns] = value.astype(jnp.bfloat16)


def fill_kernel(shots, chunks, tile, *refs):
    partner_ref, wave_ref, data_ref, permute_hbm, mask_hbm = refs[:5]
    base_hbm, factor_hbm = refs[5:7]
    out_ref = refs[7] if chunks > 1 else None
    refs = refs[8 if chunks > 1 else 7 :]
    turned, taken, permute_ref, mask_ref, base_ref, factor_ref, held, sems = refs
    stations = data_ref.shape[1]
    block = min(128, stations)
    load_permute = pltpu.make_async_copy(permute_hbm, permute_ref, sems.at[0])
    load_mask = pltpu.make_async_copy(mask_hbm, mask_ref, sems.at[1])
    load_permute.start()
    load_mask.start()
    for part in range(2):

        @pl.loop(0, stations // block)
        def _(step):
            rows = pl.ds(pl.multiple_of(step * block, block), block)
            turned[:, rows] = data_ref[part, rows, :].astype(jnp.float32).T

        @pl.loop(0, stations // (4 * BS))
        def _(step):
            for inner in range(4):
                source = pl.ds(pl.multiple_of(partner_ref[4 * step + inner] * BS, BS), BS)
                into = pl.ds(pl.multiple_of((4 * step + inner) * BS, BS), BS)
                taken[part, into, :] = turned[source, :]

    load_permute.wait()
    load_mask.wait()
    high = min(256, stations)
    size = shots // chunks
    piece = high // chunks
    wave_re = wave_ref[0]
    wave_im = wave_ref[1]

    @pl.loop(0, stations // high)
    def _(step):
        rows = pl.ds(pl.multiple_of(step * high, high), high)
        lower = pl.ds(pl.multiple_of(stations + step * high, high), high)
        pieces = pl.ds(pl.multiple_of(step * piece, piece), piece)
        present = mask_ref[rows, :].astype(jnp.float32) > 0.5
        filled = []
        for part in range(2):
            columns = slice(part * stations, (part + 1) * stations)
            mirrored = jnp.dot(
                taken[part, rows, :].astype(jnp.bfloat16),
                permute_ref[...],
                preferred_element_type=jnp.float32,
            )
            value = jnp.where(present, data_ref[part, rows, :].astype(jnp.float32), mirrored)
            filled.append(value)
            if chunks > 1:
                grouped = value.reshape(high // shots, shots, stations)
                for chunk in range(chunks):
                    own = grouped[:, chunk * size : (chunk + 1) * size]
                    base_ref[chunk, pieces, columns] = own.reshape(piece, stations).astype(
                        jnp.bfloat16
                    )
            else:
                base_ref[0, rows, columns] = value.astype(jnp.bfloat16)
        factor_re = (wave_re * filled[0] - wave_im * filled[1]).astype(jnp.bfloat16)
        factor_im = (wave_re * filled[1] + wave_im * filled[0]).astype(jnp.bfloat16)
        factor_ref[rows, :stations] = factor_re
        factor_ref[rows, stations:] = factor_im
        factor_ref[lower, :stations] = -factor_im
        factor_ref[lower, stations:] = factor_re

    store_base = pltpu.make_async_copy(base_ref, base_hbm, sems.at[2])
    store_factor = pltpu.make_async_copy(factor_ref, factor_hbm, sems.at[3])
    store_base.start()
    store_factor.start()
    if chunks > 1:
        iterate(tile, base_ref.at[0], factor_ref, out_ref, held)
    store_base.wait()
    store_factor.wait()


def fill(partner, wave, data, permute, mask, shots, chunks):
    stations = data.shape[1]
    rows = stations // chunks
    width = 2 * stations
    vmem = pl.BlockSpec(memory_space=pltpu.VMEM)
    smem = pl.BlockSpec(memory_space=pltpu.SMEM)
    hbm = pl.BlockSpec(memory_space=pl.ANY)
    out_shape = [
        jax.ShapeDtypeStruct((chunks, rows, width), jnp.bfloat16),
        jax.ShapeDtypeStruct((width, width), jnp.bfloat16),
    ]
    if chunks > 1:
        size = shots // chunks
        out_shape.append(
            jax.ShapeDtypeStruct((stations // shots, 2, size, stations), jnp.bfloat16)
        )
    return pl.pallas_call(
        lambda *refs: fill_kernel(shots, chunks, min(512, stations), *refs),
        out_shape=out_shape,
        in_specs=[smem, smem, vmem, hbm, hbm],
        out_specs=[hbm, hbm, vmem][: len(out_shape)],
        scratch_shapes=[
            pltpu.VMEM((stations, stations), jnp.float32),
            pltpu.VMEM((2, stations, stations), jnp.float32),
            pltpu.VMEM((stations, stations), jnp.bfloat16),
            pltpu.VMEM((stations, stations), jnp.bfloat16),
            pltpu.VMEM((chunks, rows, width), jnp.bfloat16),
            pltpu.VMEM((width, width), jnp.bfloat16),
            pltpu.VMEM((2, rows if chunks > 1 else 16, width), jnp.bfloat16),
            pltpu.SemaphoreType.DMA((4,)),
        ],
        compiler_params=pltpu.CompilerParams(vmem_limit_bytes=56 << 20),
        cost_estimate=pl.CostEstimate(
            flops=4 * stations**3, bytes_accessed=20 * stations**2, transcendentals=0
        ),
        name="fill",
    )(partner, wave, data, permute, mask)


def solve_kernel(tile, base_ref, factor_ref, out_ref, held):
    iterate(tile, base_ref, factor_ref, out_ref, held)


def solve(base, factor, chunk, groups):
    _, rows, width = base.shape
    stations = width // 2
    size = rows // groups
    shape = (groups, 2, size, stations) if size % 8 == 0 else (2, rows, stations)
    solved = pl.pallas_call(
        lambda *refs: solve_kernel(min(512, stations), *refs),
        grid=(1,),
        out_shape=jax.ShapeDtypeStruct(shape, jnp.bfloat16),
        in_specs=[
            pl.BlockSpec((None, rows, width), lambda i: (chunk, 0, 0)),
            pl.BlockSpec((width, width), lambda i: (0, 0), pipeline_mode=pl.Buffered(1)),
        ],
        out_specs=pl.BlockSpec(shape, lambda i: (0,) * len(shape)),
        scratch_shapes=[pltpu.VMEM((2, rows, width), jnp.bfloat16)],
        compiler_params=pltpu.CompilerParams(vmem_limit_bytes=40 << 20),
        cost_estimate=pl.CostEstimate(
            flops=2 * ITERS * rows * width * width,
            bytes_accessed=2 * (2 * rows * width + width * width),
            transcendentals=0,
        ),
        name="solve",
    )(base, factor)
    if len(shape) == 3:
        solved = jnp.swapaxes(solved.reshape(2, groups, size, stations), 0, 1)
    return solved


def restore_kernel(data_ref, table_ref, *rest):
    out_ref = rest[-1]
    for shot in range(data_ref.shape[0]):
        out_ref[shot] = lax.dot_general(
            data_ref[shot],
            table_ref[...],
            (((0,), (0,)), ((), ())),
            preferred_element_type=jnp.float32,
        ).astype(jnp.bfloat16)


def restore(data, table, whole, first, shot_count):
    count, parts, stations = data.shape
    samples = table.shape[1]
    step = math.gcd(math.gcd(4, count), first) if first else math.gcd(4, count)
    in_specs = [
        pl.BlockSpec((step, parts, stations), lambda i: (i, 0, 0)),
        pl.BlockSpec((parts, samples), lambda i: (0, 0)),
    ]
    args = [data, table]
    aliases = {}
    if whole is not None:
        in_specs.append(pl.BlockSpec(memory_space=pl.ANY))
        args.append(whole)
        aliases = {2: 0}
    return pl.pallas_call(
        restore_kernel,
        grid=(count // step,),
        out_shape=jax.ShapeDtypeStruct((shot_count, stations, samples), jnp.bfloat16),
        in_specs=in_specs,
        out_specs=pl.BlockSpec((step, stations, samples), lambda i: (first // step + i, 0, 0)),
        input_output_aliases=aliases,
        compiler_params=pltpu.CompilerParams(vmem_limit_bytes=32 << 20),
        cost_estimate=pl.CostEstimate(
            flops=2 * count * parts * stations * samples,
            bytes_accessed=2 * count * stations * (samples + parts),
            transcendentals=0,
        ),
        name="restore",
    )(*args)


def shards(recorded, acquired, partner, band_counts, wavelet):
    band_size = lax.axis_size("band")
    devices = band_size * lax.axis_size("row")
    shot_count, stations, _ = recorded.shape
    copies = devices // NF
    here = lax.axis_index("row") * band_size + lax.axis_index("band")
    forward, inverse = dft_tables()

    head = max(1, shot_count // 4)
    pieces = []
    for begin, end in ((0, head), (head, shot_count)):
        part = lax.slice_in_dim(recorded, begin, end, axis=0)
        spectra = jnp.einsum(
            "ct,srt->csr", forward, part, preferred_element_type=jnp.float32
        ).astype(jnp.bfloat16)
        spectra = jnp.swapaxes(spectra.reshape(2, NF, end - begin, stations), 0, 1)
        if copies > 1:
            spectra = jnp.repeat(spectra, copies, axis=0)
        pieces.append(lax.all_to_all(spectra, AXES, split_axis=0, concat_axis=0, tiled=True))
    data = jnp.concatenate(pieces, axis=2)
    data = jnp.swapaxes(data, 0, 1).reshape(2, stations, stations)

    offsets = jnp.arange(BS, dtype=jnp.int32)
    mirror_index = (BS * partner[:, None] + offsets[None, :]).reshape(stations)
    station = jnp.arange(stations, dtype=jnp.int32)
    permute = (station[:, None] == mirror_index[None, :]).astype(jnp.bfloat16)
    mask = jnp.repeat(jnp.repeat(acquired, BS, axis=0), BS, axis=1).astype(jnp.bfloat16)
    own_bin = here // copies
    own_group = jnp.sum((jnp.cumsum(band_counts) <= own_bin).astype(jnp.int32))
    chosen = jnp.arange(band_counts.shape[0], dtype=jnp.int32) == own_group
    rescale = 1.0 / math.sqrt(stations)
    wave = jnp.sum(chosen.astype(jnp.float32)[None] * wavelet, axis=1) * rescale
    own_count = shot_count // copies
    chunks = min(CHUNKS, own_count)
    size = own_count // chunks
    together = copies == 1 and size % 8 == 0 and chunks > 1
    made = fill(partner, wave, data, permute, mask, shot_count, chunks if together else 1)
    base, factor = made[:2]
    if not together:
        base = base.reshape(devices, shot_count, 2 * stations)
        base = lax.dynamic_slice_in_dim(base, here % copies * own_count, own_count, axis=1)
        base = jnp.swapaxes(base.reshape(devices, chunks, size, 2 * stations), 0, 1)
        base = base.reshape(chunks, devices * size, 2 * stations)
    output = None
    for chunk in range(chunks):
        if together and chunk == 0:
            solved = made[2]
        else:
            solved = solve(base, factor, chunk, devices)
        back = lax.all_to_all(solved, AXES, split_axis=0, concat_axis=0, tiled=True)
        if output is not None:
            back, output = lax.optimization_barrier((back, output))
        back = back.reshape(NF, copies, 2, size, stations)
        back = jnp.transpose(back, (1, 3, 2, 0, 4)).reshape(copies, size, 2 * NF, stations)
        for copy in range(copies):
            output = restore(
                back[copy], inverse, output, copy * own_count + chunk * size, shot_count
            )
    return output


def solution(mesh):
    return jax.shard_map(
        shards,
        mesh=mesh,
        in_specs=(P(AXES, None, None), P(), P(), P(), P()),
        out_specs=P(AXES, None, None),
        check_vma=False,
    )
```

```python
import math

import jax
import jax.numpy as jnp
import numpy as np
from jax import lax
from jax.experimental import pallas as pl
from jax.experimental.pallas import tpu as pltpu
from jax.sharding import PartitionSpec as P

NT = 512
NF = 32
FLO = 4
BS = 8
ITERS = 5
CHUNKS = 4
AXES = ("row", "band")


def dft_tables():
    sample_index = np.arange(NT, dtype=np.int32)
    bin_index = FLO + np.arange(NF, dtype=np.int32)
    angles = (bin_index[:, None] * sample_index[None, :] % NT).astype(np.float32) * np.float32(
        2.0 * math.pi / NT
    )
    cycles = np.concatenate([np.cos(angles), -np.sin(angles)], axis=0)
    forward = cycles * np.float32(1.0 / math.sqrt(NT))
    inverse = cycles * np.float32(math.sqrt(2.0 / NF))
    return (jnp.asarray(forward, jnp.bfloat16), jnp.asarray(inverse, jnp.bfloat16))


def iterate(tile, base_ref, factor_ref, out_ref, held):
    width = base_ref.shape[1]
    half = width // 2
    for turn in range(ITERS):
        left = base_ref if turn == 0 else held.at[(turn + 1) % 2]

        @pl.loop(0, width // tile)
        def _(step):
            columns = pl.ds(pl.multiple_of(step * tile, tile), tile)
            product = jnp.dot(
                left[...], factor_ref[:, columns], preferred_element_type=jnp.float32
            )
            value = base_ref[:, columns].astype(jnp.float32) - product
            if turn == ITERS - 1:
                inside = pl.ds(pl.multiple_of(step * tile % half, tile), tile)
                part = step * tile // half
                if len(out_ref.shape) == 4:
                    groups, _, size, _ = out_ref.shape
                    value = value.reshape(groups, size, tile)
                    out_ref[:, part, :, inside] = value.astype(jnp.bfloat16)
                else:
                    out_ref[part, :, inside] = value.astype(jnp.bfloat16)
            else:
                held[turn % 2, :, columns] = value.astype(jnp.bfloat16)


def source_rows(data_ref, part, step, count):
    shots, stations = data_ref.shape[2:]
    sources = pl.ds(step * (count // shots), count // shots)
    return data_ref[sources, part].astype(jnp.float32).reshape(count, stations)


def fill_kernel(shots, chunks, tile, *refs):
    partner_ref, wave_ref, data_ref, permute_hbm, mask_hbm = refs[:5]
    base_hbm, factor_hbm = refs[5:7]
    out_ref = refs[7] if chunks > 1 else None
    refs = refs[8 if chunks > 1 else 7 :]
    turned, taken, permute_ref, mask_ref, base_ref, factor_ref, held, sems = refs
    stations = data_ref.shape[3]
    block = min(128, stations)
    load_permute = pltpu.make_async_copy(permute_hbm, permute_ref, sems.at[0])
    load_mask = pltpu.make_async_copy(mask_hbm, mask_ref, sems.at[1])
    load_permute.start()
    load_mask.start()
    for part in range(2):

        @pl.loop(0, stations // block)
        def _(step):
            rows = pl.ds(pl.multiple_of(step * block, block), block)
            turned[:, rows] = source_rows(data_ref, part, step, block).T

        @pl.loop(0, stations // (4 * BS))
        def _(step):
            for inner in range(4):
                source = pl.ds(pl.multiple_of(partner_ref[4 * step + inner] * BS, BS), BS)
                into = pl.ds(pl.multiple_of((4 * step + inner) * BS, BS), BS)
                taken[part, into, :] = turned[source, :]

    load_permute.wait()
    load_mask.wait()
    high = min(256, stations)
    size = shots // chunks
    piece = high // chunks
    wave_re = wave_ref[0]
    wave_im = wave_ref[1]

    @pl.loop(0, stations // high)
    def _(step):
        rows = pl.ds(pl.multiple_of(step * high, high), high)
        lower = pl.ds(pl.multiple_of(stations + step * high, high), high)
        pieces = pl.ds(pl.multiple_of(step * piece, piece), piece)
        present = mask_ref[rows, :].astype(jnp.float32) > 0.5
        filled = []
        for part in range(2):
            columns = slice(part * stations, (part + 1) * stations)
            mirrored = jnp.dot(
                taken[part, rows, :].astype(jnp.bfloat16),
                permute_ref[...],
                preferred_element_type=jnp.float32,
            )
            value = jnp.where(present, source_rows(data_ref, part, step, high), mirrored)
            filled.append(value)
            if chunks > 1:
                grouped = value.reshape(high // shots, shots, stations)
                for chunk in range(chunks):
                    own = grouped[:, chunk * size : (chunk + 1) * size]
                    base_ref[chunk, pieces, columns] = own.reshape(piece, stations).astype(
                        jnp.bfloat16
                    )
            else:
                base_ref[0, rows, columns] = value.astype(jnp.bfloat16)
        factor_re = (wave_re * filled[0] - wave_im * filled[1]).astype(jnp.bfloat16)
        factor_im = (wave_re * filled[1] + wave_im * filled[0]).astype(jnp.bfloat16)
        factor_ref[rows, :stations] = factor_re
        factor_ref[rows, stations:] = factor_im
        factor_ref[lower, :stations] = -factor_im
        factor_ref[lower, stations:] = factor_re

    store_base = pltpu.make_async_copy(base_ref, base_hbm, sems.at[2])
    store_factor = pltpu.make_async_copy(factor_ref, factor_hbm, sems.at[3])
    store_base.start()
    store_factor.start()
    if chunks > 1:
        iterate(tile, base_ref.at[0], factor_ref, out_ref, held)
    store_base.wait()
    store_factor.wait()


def fill(partner, wave, data, permute, mask, shots, chunks):
    stations = data.shape[3]
    rows = stations // chunks
    width = 2 * stations
    vmem = pl.BlockSpec(memory_space=pltpu.VMEM)
    smem = pl.BlockSpec(memory_space=pltpu.SMEM)
    hbm = pl.BlockSpec(memory_space=pl.ANY)
    out_shape = [
        jax.ShapeDtypeStruct((chunks, rows, width), jnp.bfloat16),
        jax.ShapeDtypeStruct((width, width), jnp.bfloat16),
    ]
    if chunks > 1:
        size = shots // chunks
        out_shape.append(
            jax.ShapeDtypeStruct((stations // shots, 2, size, stations), jnp.bfloat16)
        )
    return pl.pallas_call(
        lambda *refs: fill_kernel(shots, chunks, min(512, stations), *refs),
        out_shape=out_shape,
        in_specs=[smem, smem, vmem, hbm, hbm],
        out_specs=[hbm, hbm, vmem][: len(out_shape)],
        scratch_shapes=[
            pltpu.VMEM((stations, stations), jnp.float32),
            pltpu.VMEM((2, stations, stations), jnp.float32),
            pltpu.VMEM((stations, stations), jnp.bfloat16),
            pltpu.VMEM((stations, stations), jnp.bfloat16),
            pltpu.VMEM((chunks, rows, width), jnp.bfloat16),
            pltpu.VMEM((width, width), jnp.bfloat16),
            pltpu.VMEM((2, rows if chunks > 1 else 16, width), jnp.bfloat16),
            pltpu.SemaphoreType.DMA((4,)),
        ],
        compiler_params=pltpu.CompilerParams(vmem_limit_bytes=56 << 20),
        cost_estimate=pl.CostEstimate(
            flops=4 * stations**3, bytes_accessed=20 * stations**2, transcendentals=0
        ),
        name="fill",
    )(partner, wave, data, permute, mask)


def solve_kernel(tile, base_ref, factor_ref, out_ref, held):
    iterate(tile, base_ref, factor_ref, out_ref, held)


def solve(base, factor, chunk, groups):
    _, rows, width = base.shape
    stations = width // 2
    size = rows // groups
    shape = (groups, 2, size, stations) if size % 8 == 0 else (2, rows, stations)
    solved = pl.pallas_call(
        lambda *refs: solve_kernel(min(512, stations), *refs),
        grid=(1,),
        out_shape=jax.ShapeDtypeStruct(shape, jnp.bfloat16),
        in_specs=[
            pl.BlockSpec((None, rows, width), lambda i: (chunk, 0, 0)),
            pl.BlockSpec((width, width), lambda i: (0, 0), pipeline_mode=pl.Buffered(1)),
        ],
        out_specs=pl.BlockSpec(shape, lambda i: (0,) * len(shape)),
        scratch_shapes=[pltpu.VMEM((2, rows, width), jnp.bfloat16)],
        compiler_params=pltpu.CompilerParams(vmem_limit_bytes=40 << 20),
        cost_estimate=pl.CostEstimate(
            flops=2 * ITERS * rows * width * width,
            bytes_accessed=2 * (2 * rows * width + width * width),
            transcendentals=0,
        ),
        name="solve",
    )(base, factor)
    if len(shape) == 3:
        solved = jnp.swapaxes(solved.reshape(2, groups, size, stations), 0, 1)
    return solved


def restore_kernel(data_ref, table_ref, *rest):
    out_ref = rest[-1]
    for shot in range(data_ref.shape[0]):
        out_ref[shot] = lax.dot_general(
            data_ref[shot],
            table_ref[...],
            (((0,), (0,)), ((), ())),
            preferred_element_type=jnp.float32,
        ).astype(jnp.bfloat16)


def restore(data, table, whole, first, shot_count):
    count, parts, stations = data.shape
    samples = table.shape[1]
    step = math.gcd(math.gcd(4, count), first) if first else math.gcd(4, count)
    in_specs = [
        pl.BlockSpec((step, parts, stations), lambda i: (i, 0, 0)),
        pl.BlockSpec((parts, samples), lambda i: (0, 0)),
    ]
    args = [data, table]
    aliases = {}
    if whole is not None:
        in_specs.append(pl.BlockSpec(memory_space=pl.ANY))
        args.append(whole)
        aliases = {2: 0}
    return pl.pallas_call(
        restore_kernel,
        grid=(count // step,),
        out_shape=jax.ShapeDtypeStruct((shot_count, stations, samples), jnp.bfloat16),
        in_specs=in_specs,
        out_specs=pl.BlockSpec((step, stations, samples), lambda i: (first // step + i, 0, 0)),
        input_output_aliases=aliases,
        compiler_params=pltpu.CompilerParams(vmem_limit_bytes=32 << 20),
        cost_estimate=pl.CostEstimate(
            flops=2 * count * parts * stations * samples,
            bytes_accessed=2 * count * stations * (samples + parts),
            transcendentals=0,
        ),
        name="restore",
    )(*args)


def shards(recorded, acquired, partner, band_counts, wavelet):
    band_size = lax.axis_size("band")
    devices = band_size * lax.axis_size("row")
    shot_count, stations, _ = recorded.shape
    copies = devices // NF
    here = lax.axis_index("row") * band_size + lax.axis_index("band")
    forward, inverse = dft_tables()

    head = max(1, shot_count // 4)
    pieces = []
    for begin, end in ((0, head), (head, shot_count)):
        part = lax.slice_in_dim(recorded, begin, end, axis=0)
        spectra = jnp.einsum(
            "ct,srt->csr", forward, part, preferred_element_type=jnp.float32
        ).astype(jnp.bfloat16)
        spectra = jnp.swapaxes(spectra.reshape(2, NF, end - begin, stations), 0, 1)
        if copies > 1:
            spectra = jnp.repeat(spectra, copies, axis=0)
        pieces.append(lax.all_to_all(spectra, AXES, split_axis=0, concat_axis=0, tiled=True))
    data = jnp.concatenate(pieces, axis=2)

    offsets = jnp.arange(BS, dtype=jnp.int32)
    mirror_index = (BS * partner[:, None] + offsets[None, :]).reshape(stations)
    station = jnp.arange(stations, dtype=jnp.int32)
    permute = (station[:, None] == mirror_index[None, :]).astype(jnp.bfloat16)
    mask = jnp.repeat(jnp.repeat(acquired, BS, axis=0), BS, axis=1).astype(jnp.bfloat16)
    own_bin = here // copies
    own_group = jnp.sum((jnp.cumsum(band_counts) <= own_bin).astype(jnp.int32))
    chosen = jnp.arange(band_counts.shape[0], dtype=jnp.int32) == own_group
    rescale = 1.0 / math.sqrt(stations)
    wave = jnp.sum(chosen.astype(jnp.float32)[None] * wavelet, axis=1) * rescale
    own_count = shot_count // copies
    chunks = min(CHUNKS, own_count)
    size = own_count // chunks
    together = copies == 1 and size % 8 == 0 and chunks > 1
    made = fill(partner, wave, data, permute, mask, shot_count, chunks if together else 1)
    base, factor = made[:2]
    if not together:
        base = base.reshape(devices, shot_count, 2 * stations)
        base = lax.dynamic_slice_in_dim(base, here % copies * own_count, own_count, axis=1)
        base = jnp.swapaxes(base.reshape(devices, chunks, size, 2 * stations), 0, 1)
        base = base.reshape(chunks, devices * size, 2 * stations)
    output = None
    for chunk in range(chunks):
        if together and chunk == 0:
            solved = made[2]
        else:
            solved = solve(base, factor, chunk, devices)
        back = lax.all_to_all(solved, AXES, split_axis=0, concat_axis=0, tiled=True)
        if output is not None:
            back, output = lax.optimization_barrier((back, output))
        back = back.reshape(NF, copies, 2, size, stations)
        back = jnp.transpose(back, (1, 3, 2, 0, 4)).reshape(copies, size, 2 * NF, stations)
        for copy in range(copies):
            output = restore(
                back[copy], inverse, output, copy * own_count + chunk * size, shot_count
            )
    return output


def solution(mesh):
    return jax.shard_map(
        shards,
        mesh=mesh,
        in_specs=(P(AXES, None, None), P(), P(), P(), P()),
        out_specs=P(AXES, None, None),
        check_vma=False,
    )
```
